256 devices in a mesh: rec: 8 (over y, core), tm: 32 (over x, z).
Axes of the slice: x: 4, y: 4, z: 8, core: 2. Of those that a mesh axis runs over, the one named last changes fastest.
Arguments:
- normed: bfloat16 [8, 1024, 4096], P('rec', None, 'tm'), may hold values from -6 to 6
- query_act: bfloat16 [8, 1024, 4096], P('rec', None, 'tm'), may hold values from -16 to 16
- key_act: bfloat16 [8, 1024, 4096], P('rec', None, 'tm'), may hold values from -16 to 16
- value_act: bfloat16 [8, 1024, 4096], P('rec', None, 'tm'), may hold values from -6 to 6
- grad_out: bfloat16 [8, 1024, 4096], P('rec', None, 'tm'), may hold values from -12 to 12
- w_qkv: bfloat16 [1024, 3072], replicated, may hold values from -0.1875 to 0.1875
- w_out: bfloat16 [1024, 1024], replicated, may hold values from -0.1875 to 0.1875
- lengths: int32 [8], P('rec'), may hold values from 512 to 1048576, as said below
- offsets: int32 [8], P('rec'), may hold values from 0 to 1040384
Outputs:
- grad_normed: bfloat16 [8, 1024, 4096], P('rec', None, 'tm')
- dw_qkv: float32 [1024, 3072], P('tm')
- dw_out: float32 [1024, 1024], P('tm')
The draws below stay inside these ranges and needn't reach their ends.
Inputs may be any that keep to these rules, and one draw needn't show every extreme that they name: lengths - offsets is 512 or more for every recording, and 4096 or more for at least one recording; some recording's window ends a recording of the longest length.
All inputs are finite; a program needn't handle non-finite values.
Results may differ from the reference program's by a relative error of at most 0.035.
Values may be sent and summed in bfloat16 or wider, within the bound.
No kernel may reach another device: no remote copies, remote signals or barrier semaphores. Data moves between devices by JAX's collectives and lax.ppermute only.
A program may use at most 128 MiB of HBM per device.

```python
import math
import jax
import jax.numpy as jnp
from jax import lax

D = 1024
HEADS = 32
WINDOW = 1024
QBLOCK = 512
REC = 8
SEQ = 4096


frame_limit = 1048576


def saved_pair(key, align_rate):
    full_shape = (REC, D, SEQ)
    pair = []
    for salt_value in (31, 32):
        normal_vals = jnp.clip(jax.random.normal(jax.random.fold_in(key, salt_value), full_shape, jnp.float32), -6.0, 6.0)
        pair.append(normal_vals)
    chosen = jax.random.uniform(jax.random.fold_in(key, 51), (REC, 1, SEQ), jnp.float32) < align_rate
    target = jax.random.uniform(jax.random.fold_in(key, 52), (REC, 1, SEQ), jnp.float32, 120.0, 420.0)
    level = jnp.sqrt(target / math.sqrt(D // HEADS))
    signs = jnp.where(jax.random.uniform(jax.random.fold_in(key, 53), full_shape, jnp.float32) < 0.5, 1.0, -1.0)
    aligned = level * signs
    gap_size = jax.random.uniform(jax.random.fold_in(key, 54), (REC, 1, SEQ), jnp.float32, 1.5, 2.5)
    nearby = aligned * (1.0 - gap_size / target)
    queries = jnp.where(chosen, aligned, pair[0])
    keys_out = jnp.where(jnp.roll(chosen, -1, axis=2), jnp.roll(nearby, -1, axis=2), pair[1])
    keys_out = jnp.where(chosen, aligned, keys_out)
    return (queries, keys_out)


def draw_query_act(key, part):
    return saved_pair(key, 0.0)[0].astype(jnp.bfloat16)


def draw_key_act(key, part):
    return saved_pair(key, 0.0)[1].astype(jnp.bfloat16)


def window_bounds(key):
    short_live = jax.random.randint(jax.random.fold_in(key, 61), (REC,), SEQ // 8, SEQ)
    whole = jax.random.randint(jax.random.fold_in(key, 62), (REC,), 0, 3) == 0
    picked = jax.random.randint(jax.random.fold_in(key, 63), (), 0, REC)
    is_picked = jnp.arange(REC, dtype=jnp.int32) == picked
    whole = whole | is_picked
    beyond = jax.random.randint(jax.random.fold_in(key, 64), (REC,), SEQ, 2 * SEQ + 1)
    live_count = jnp.where(whole, beyond, short_live)
    live_count = jnp.where(is_picked, 2 * SEQ, live_count)
    starts = jax.random.randint(jax.random.fold_in(key, 65), (REC,), 0, frame_limit - 2 * SEQ + 1)
    starts = jnp.where(is_picked, frame_limit - 2 * SEQ, starts)
    return (starts.astype(jnp.int32), (starts + live_count).astype(jnp.int32))


def draw_lengths(key, part):
    return window_bounds(key)[1]


def draw_offsets(key, part):
    return window_bounds(key)[0]


def strengthened(array, stream_key, source, target, blocks, factor):
    owner, partner = [(jnp.arange(array.shape[position]) // (array.shape[position] // blocks)).reshape([-1 if axis == position else 1 for axis in range(array.ndim)]) for position in (source, target)]
    chosen = jax.random.permutation(stream_key, blocks)[partner]
    strong = (owner == chosen) | (owner == (partner + blocks // 2) % blocks)
    return jnp.where(strong, factor * array, array)


def levels(own_key, dims, pieces, smallest, top_value):
    factor_of = 1.0
    for position, parts in pieces:
        draws = jax.random.uniform(jax.random.fold_in(jax.random.fold_in(own_key, 6), position), (parts,), jnp.float32, smallest / len(pieces), top_value / len(pieces))
        factor_of = factor_of * jnp.repeat(jnp.exp(draws), dims[position] // parts).reshape((-1,) + (1,) * (len(dims) - 1 - position))
    return factor_of


def centred(rng, shape, width, reach, shards=(), kind=jnp.bfloat16):
    drawn = width * jax.random.normal(rng, shape, jnp.float32)
    if shards:
        drawn = drawn * levels(rng, shape, shards, -0.22, 0.18)
    return jnp.clip(drawn, -reach, reach).astype(kind)


def bell_draw_with(rng, extent, deviation, reach, pieces, heavy, kind=jnp.bfloat16):
    result = deviation * jax.random.normal(rng, extent, jnp.float32)
    if pieces:
        result = result * levels(rng, extent, pieces, -0.22, 0.18)
    return jnp.clip(strengthened(result, jax.random.fold_in(rng, 3), *heavy), -reach, reach).astype(kind)


def setup_inputs(seed: int = 0) -> dict:
    arg_keys = jax.random.split(jax.random.key(seed), 10)
    return {
        "normed": centred(arg_keys[0], (REC, D, SEQ), 1.0, 6.0, ((0, 8), (2, 32))),
        "query_act": draw_query_act(jax.random.fold_in(arg_keys[9], 71), 0),
        "key_act": draw_key_act(jax.random.fold_in(arg_keys[9], 71), 0),
        "value_act": centred(arg_keys[3], (REC, D, SEQ), 1.0, 6.0, ((0, 8), (2, 32))),
        "grad_out": bell_draw_with(arg_keys[4], (REC, D, SEQ), 2.0, 12.0, ((0, 8), (2, 32)), (2, 1, 32, 2.75)),
        "w_qkv": centred(arg_keys[5], (D, 3 * D), D ** -0.5, 0.1875),
        "w_out": centred(arg_keys[6], (D, D), D ** -0.5, 0.1875),
        "lengths": draw_lengths(jax.random.fold_in(arg_keys[9], 71), 0),
        "offsets": draw_offsets(jax.random.fold_in(arg_keys[9], 71), 0),
    }


masked_score = -1e+30

def block_terms(q_blk, g_blk, key_span, value_span, block_start, live_frames, score_scale):
    half_window = WINDOW // 2
    row_ids = block_start + jnp.arange(QBLOCK, dtype=jnp.int32)
    col_ids = block_start - half_window + jnp.arange(QBLOCK + WINDOW, dtype=jnp.int32)
    visible = (col_ids[None, :] >= 0) & (col_ids[None, :] < live_frames) & (jnp.abs(row_ids[:, None] - col_ids[None, :]) < half_window)
    query_live = (row_ids < live_frames).astype(jnp.float32)
    scores = jnp.einsum('hdq,hdk->hqk', q_blk.astype(jnp.float32), key_span.astype(jnp.float32)) * score_scale
    scores = jnp.where(visible[None], scores, masked_score)
    row_max = lax.optimization_barrier(jnp.max(scores, axis=2, keepdims=True))
    exponent = jnp.exp(scores - row_max)
    prob = exponent / lax.optimization_barrier(jnp.sum(exponent, axis=2, keepdims=True)) * query_live[None, :, None]
    prob_b = prob.astype(jnp.bfloat16)
    attn_out = jnp.einsum('hqk,hdk->hdq', prob_b.astype(jnp.float32), value_span.astype(jnp.float32)).astype(jnp.bfloat16)
    row_dot = lax.optimization_barrier(jnp.sum(g_blk.astype(jnp.float32) * attn_out.astype(jnp.float32), axis=1))
    prob_grad = jnp.einsum('hdq,hdk->hqk', g_blk.astype(jnp.float32), value_span.astype(jnp.float32))
    dscore = (prob * (prob_grad - row_dot[:, :, None])).astype(jnp.bfloat16)
    grad_q = jnp.einsum('hqk,hdk->hdq', dscore.astype(jnp.float32), key_span.astype(jnp.float32)) * score_scale
    grad_k = jnp.einsum('hqk,hdq->hdk', dscore.astype(jnp.float32), q_blk.astype(jnp.float32)) * score_scale
    grad_v = jnp.einsum('hqk,hdq->hdk', prob_b.astype(jnp.float32), g_blk.astype(jnp.float32))
    return (attn_out, grad_q.astype(jnp.bfloat16), grad_k, grad_v)

def window_attention(queries, key_set, values, head_grad, live_frames):
    head_count, head_dim, seq_len = queries.shape
    score_scale = 1.0 / math.sqrt(head_dim)
    half_window = WINDOW // 2
    span = QBLOCK + WINDOW
    pad_cfg = ((0, 0), (0, 0), (half_window, half_window))
    key_pad = jnp.pad(key_set, pad_cfg)
    value_pad = jnp.pad(values, pad_cfg)
    zero_acc = jnp.zeros((head_count, head_dim, seq_len + WINDOW), jnp.float32)

    def step(accums, block_index):
        key_acc, value_acc = accums
        block_start = (block_index * QBLOCK).astype(jnp.int32)
        q_blk = lax.dynamic_slice_in_dim(queries, block_start, QBLOCK, 2)
        g_blk = lax.dynamic_slice_in_dim(head_grad, block_start, QBLOCK, 2)
        key_span = lax.dynamic_slice_in_dim(key_pad, block_start, span, 2)
        value_span = lax.dynamic_slice_in_dim(value_pad, block_start, span, 2)
        attn_out, grad_q, grad_k, grad_v = block_terms(q_blk, g_blk, key_span, value_span, block_start, live_frames, score_scale)
        key_acc = lax.dynamic_update_slice_in_dim(key_acc, lax.dynamic_slice_in_dim(key_acc, block_start, span, 2) + grad_k, block_start, 2)
        value_acc = lax.dynamic_update_slice_in_dim(value_acc, lax.dynamic_slice_in_dim(value_acc, block_start, span, 2) + grad_v, block_start, 2)
        return ((key_acc, value_acc), (attn_out, grad_q))
    (key_acc, value_acc), (outs, grads) = lax.scan(step, (zero_acc, zero_acc), jnp.arange(seq_len // QBLOCK, dtype=jnp.int32))

    def unblock(blocked):
        return jnp.transpose(blocked, (1, 2, 0, 3)).reshape(head_count, head_dim, seq_len)
    grad_key = key_acc[:, :, half_window:half_window + seq_len].astype(jnp.bfloat16)
    grad_value = value_acc[:, :, half_window:half_window + seq_len].astype(jnp.bfloat16)
    return (unblock(outs), unblock(grads), grad_key, grad_value)

def reference(normed, query_act, key_act, value_act, grad_out, w_qkv, w_out, lengths, offsets):
    head_dim = D // HEADS
    grad_rows = []
    dw_qkv = jnp.zeros((D, 3 * D), jnp.float32)
    dw_out = jnp.zeros((D, D), jnp.float32)
    w_three = w_qkv.reshape(D, 3, D)
    for record in range(REC):
        live_frames = jnp.clip(lengths[record] - offsets[record], 0, SEQ).astype(jnp.int32)
        head_grad = jnp.dot(w_out.T, grad_out[record], preferred_element_type=jnp.float32).astype(jnp.bfloat16)

        def per_head(group_acts):
            return window_attention(group_acts[0], group_acts[1], group_acts[2], group_acts[3], live_frames)
        stacked = tuple((act.reshape(HEADS, 1, head_dim, SEQ) for act in (query_act[record], key_act[record], value_act[record], head_grad)))
        attn_out, grad_q, grad_k, grad_v = lax.map(per_head, stacked)
        attn_out = attn_out.reshape(D, SEQ)
        grad_q = grad_q.reshape(D, SEQ)
        grad_k = grad_k.reshape(D, SEQ)
        grad_v = grad_v.reshape(D, SEQ)
        grad_stack = jnp.stack([grad_q, grad_k, grad_v])
        grad_total = jnp.einsum('rwf,wrt->ft', w_three.astype(jnp.float32), grad_stack.astype(jnp.float32))
        grad_rows.append(grad_total.astype(jnp.bfloat16))
        dw_qkv = dw_qkv + jnp.concatenate([jnp.dot(piece, normed[record].T, preferred_element_type=jnp.float32) for piece in (grad_q, grad_k, grad_v)], axis=1)
        dw_out = dw_out + jnp.dot(grad_out[record], attn_out.T, preferred_element_type=jnp.float32)
    return (jnp.stack(grad_rows), dw_qkv, dw_out)
```

```python
import math

import jax
import jax.numpy as jnp
from jax import lax
from jax.experimental import pallas as pl
from jax.experimental.pallas import tpu as pltpu
from jax.sharding import Mesh, PartitionSpec as P

HEAD_DIM = 32
HALF = 512
QT = 256
BLK = 128
masked_score = -1e30

def attn_kernel(live_ref, x_ref, out_ref, kv_t, k_p, v_p, acc):
    blocks = x_ref.shape[0]
    seq = blocks * BLK
    span = QT + 2 * HALF
    scale = 1.0 / math.sqrt(HEAD_DIM)
    live = live_ref[0]
    f32, bf = jnp.float32, jnp.bfloat16

    zpad = jnp.zeros((HALF, BLK), bf)
    dead = jnp.where(lax.broadcasted_iota(jnp.int32, (HALF, BLK), 1) == HEAD_DIM, masked_score, 0.0).astype(bf)
    kv_t[0:HALF, :] = dead
    kv_t[HALF + seq :, :] = dead
    zl = jnp.zeros((HEAD_DIM, HALF), bf)
    for ref in (k_p, v_p):
        ref[:, 0:HALF] = zl
        ref[:, HALF + seq :] = zl
    acc[...] = jnp.zeros_like(acc)
    row_frame = lax.broadcasted_iota(jnp.int32, (HEAD_DIM, BLK), 1)
    row_id = lax.broadcasted_iota(jnp.int32, (HEAD_DIM, BLK), 0)

    def prep(b, _):
        start = pl.multiple_of(HALF + b * BLK, BLK)
        k_blk = x_ref[b, HEAD_DIM : 2 * HEAD_DIM, :]
        v_blk = x_ref[b, 2 * HEAD_DIM : 3 * HEAD_DIM, :]
        k_p[:, pl.ds(start, BLK)] = k_blk
        v_p[:, pl.ds(start, BLK)] = v_blk
        bias = jnp.where((row_id == 0) & (row_frame + b * BLK >= live), masked_score, 0.0)
        wide = jnp.concatenate(
            [k_blk.astype(f32), bias, v_blk.astype(f32), jnp.zeros((HEAD_DIM, BLK), f32)], axis=0
        )
        kv_t[pl.ds(start, BLK), :] = wide.T.astype(bf)
        return 0

    lax.fori_loop(0, blocks, prep, 0)

    b_id = lax.broadcasted_iota(jnp.int32, (QT, QT), 0)
    a_id = lax.broadcasted_iota(jnp.int32, (QT, QT), 1)
    ones_row = jnp.where(lax.broadcasted_iota(jnp.int32, (HEAD_DIM, QT), 0) == 0, 1.0, 0.0).astype(bf)
    z64 = jnp.zeros((2 * HEAD_DIM, QT), bf)
    z32 = jnp.zeros((HEAD_DIM, QT), bf)
    c = scale * math.log2(math.e)

    def dot(a, b):
        return jnp.dot(a, b, preferred_element_type=f32)

    def tile(i, _):
        base = pl.multiple_of(i * QT, QT)
        x0 = x_ref[2 * i]
        x1 = x_ref[2 * i + 1]
        q = jnp.concatenate([x0[0:32], x1[0:32]], axis=1)
        g = jnp.concatenate([x0[96:128], x1[96:128]], axis=1)
        rhs_s = jnp.concatenate([q, ones_row, z64], axis=0)
        rhs_g = jnp.concatenate([z64, g, z32], axis=0)
        kv = kv_t[pl.ds(base, span), :]
        s = dot(kv, rhs_s)
        below = b_id > a_id
        above = b_id < a_id
        edge = jnp.where(below, s[0:QT], jnp.where(above, s[span - QT :], masked_score))
        mid = s[QT : span - QT]
        m = jnp.maximum(jnp.max(mid, axis=0, keepdims=True), jnp.max(edge, axis=0, keepdims=True))
        mid = jnp.exp2((mid - m) * c)
        edge = jnp.exp2((edge - m) * c)
        total = jnp.sum(mid, axis=0, keepdims=True) + jnp.sum(edge, axis=0, keepdims=True)
        q_live = base + lax.broadcasted_iota(jnp.int32, (1, QT), 1) < live
        inv = jnp.where(q_live, 1.0 / total, 0.0)
        mid = mid * inv
        edge = edge * inv
        p = jnp.concatenate(
            [
                jnp.where(below, edge, 0.0).astype(bf),
                mid.astype(bf),
                jnp.where(above, edge, 0.0).astype(bf),
            ],
            axis=0,
        )
        ao = dot(v_p[:, pl.ds(base, span)], p).astype(bf)
        rd = jnp.sum(g.astype(f32) * ao.astype(f32), axis=0, keepdims=True)
        pg = dot(kv, rhs_g)
        d_mid = mid * (pg[QT : span - QT] - rd)
        d_edge = edge * (jnp.where(below, pg[0:QT], pg[span - QT :]) - rd)
        ds = jnp.concatenate(
            [
                jnp.where(below, d_edge, 0.0).astype(bf),
                d_mid.astype(bf),
                jnp.where(above, d_edge, 0.0).astype(bf),
            ],
            axis=0,
        )
        gq = (dot(k_p[:, pl.ds(base, span)], ds) * scale).astype(bf)
        acc[pl.ds(base, span), :] += dot(ds, rhs_s.T) + dot(p, rhs_g.T)
        for half in range(2):
            sl = slice(half * BLK, (half + 1) * BLK)
            out_ref[2 * i + half, 0:32, :] = gq[:, sl]
            out_ref[2 * i + half, 96:128, :] = ao[:, sl]
        return 0

    lax.fori_loop(0, seq // QT, tile, 0)

    def flush(b, _):
        start = pl.multiple_of(HALF + b * BLK, BLK)
        t = acc[pl.ds(start, BLK), :].T
        out_ref[b, 32:64, :] = (t[0:32] * scale).astype(bf)
        out_ref[b, 64:96, :] = t[64:96].astype(bf)
        return 0

    lax.fori_loop(0, blocks, flush, 0)

def attention(x, live):
    blocks = x.shape[0]
    seq = blocks * BLK
    padded = seq + 2 * HALF
    return pl.pallas_call(
        attn_kernel,
        out_shape=jax.ShapeDtypeStruct(x.shape, jnp.bfloat16),
        in_specs=[pl.BlockSpec(memory_space=pltpu.SMEM), pl.BlockSpec(memory_space=pltpu.VMEM)],
        out_specs=pl.BlockSpec(memory_space=pltpu.VMEM),
        scratch_shapes=[
            pltpu.VMEM((padded, BLK), jnp.bfloat16),
            pltpu.VMEM((HEAD_DIM, padded), jnp.bfloat16),
            pltpu.VMEM((HEAD_DIM, padded), jnp.bfloat16),
            pltpu.VMEM((padded, BLK), jnp.float32),
        ],
        compiler_params=pltpu.CompilerParams(vmem_limit_bytes=40 << 20),
        cost_estimate=pl.CostEstimate(flops=6 * 2 * seq * 1280 * 32, bytes_accessed=2 * x.size * 2, transcendentals=seq * 1024),
        name="window_attention",
    )(live, x)


REC_AXES = ("y", "core")
FRAME_AXES = ("x", "z")


def weight_grads(stage, normed_slice, grad_slice):
    f32, bf = jnp.float32, jnp.bfloat16
    nx, nz = stage.shape[0], stage.shape[1]
    rows = 3 * HEAD_DIM
    width = normed_slice.shape[1]
    dwq = jnp.einsum(
        "xzrt,zft->xrf", stage[:, :, :rows], normed_slice, preferred_element_type=f32
    ).astype(bf)
    dwo = jnp.einsum(
        "zct,xzdt->cxd", grad_slice, stage[:, :, rows:], preferred_element_type=f32
    ).astype(bf)
    recs = lax.axis_size(REC_AXES)
    cols = width // recs
    sub = width // (nx * nz * recs)
    send = jnp.concatenate(
        [
            dwq.reshape(nx, rows, recs, cols).transpose(2, 0, 1, 3),
            dwo.reshape(nx, nz, recs, sub, nx * HEAD_DIM)
            .transpose(2, 0, 1, 3, 4)
            .reshape(recs, nx, nz * sub, nx * HEAD_DIM),
        ],
        axis=2,
    ).reshape(recs * nx, rows + nz * sub, cols)
    terms = lax.all_to_all(send, REC_AXES + ("x",), 0, 0, tiled=True)
    summed = jnp.sum(terms.astype(f32), axis=0).astype(bf)
    out_part = lax.all_to_all(
        summed[rows:].reshape(nz, sub, nx * HEAD_DIM), "z", 0, 0, tiled=True
    ).reshape(nz * sub, nx * HEAD_DIM)
    full = lax.all_gather(jnp.concatenate([summed[:rows], out_part], axis=0), REC_AXES)
    full = full.astype(f32)
    dw_qkv = (
        full[:, :rows]
        .reshape(recs, 3, HEAD_DIM, cols)
        .transpose(2, 1, 0, 3)
        .reshape(HEAD_DIM, 3 * width)
    )
    dw_out = (
        full[:, rows:]
        .reshape(recs, nz, sub, nx, HEAD_DIM)
        .transpose(0, 2, 3, 1, 4)
        .reshape(recs * sub, width)
    )
    return dw_qkv, dw_out


def body(normed, query_act, key_act, value_act, grad_out, w_qkv, w_out, lengths, offsets):
    f32, bf = jnp.float32, jnp.bfloat16
    nx, nz = lax.axis_size("x"), lax.axis_size("z")
    shards = nx * nz
    width = w_out.shape[0]
    frames = normed.shape[2]
    seq_len = frames * shards
    live = jnp.clip(lengths - offsets, 0, seq_len).astype(jnp.int32)
    own_input = normed[0]
    own_grad = grad_out[0]
    head_grad = lax.dot_general(
        w_out, own_grad, (((0,), (0,)), ((), ())), preferred_element_type=f32
    ).astype(bf)
    sent = jnp.concatenate(
        [a.reshape(shards, HEAD_DIM, frames) for a in (query_act[0], key_act[0], value_act[0], head_grad)],
        axis=1,
    )
    heads = lax.all_to_all(sent, FRAME_AXES, 0, 0, tiled=True)
    normed_slice = lax.all_gather(own_input, "z")
    grad_slice = lax.all_gather(own_grad, "z")
    grads = attention(heads, live)
    rows = 4 * HEAD_DIM
    stage = lax.all_to_all(grads.reshape(nx, nz, rows, frames), "x", 0, 0, tiled=True)
    back = lax.all_to_all(
        stage[:, :, : 3 * HEAD_DIM].transpose(1, 0, 2, 3), "z", 0, 0, tiled=True
    )
    back = back.reshape(nz, nx, 3, HEAD_DIM, frames).transpose(2, 1, 0, 3, 4).reshape(3, width, frames)
    total = sum(
        lax.dot_general(
            w_qkv[:, i * width : (i + 1) * width],
            back[i],
            (((0,), (0,)), ((), ())),
            preferred_element_type=f32,
        )
        for i in range(3)
    )
    grad_normed = total.astype(bf)[None]
    dw_qkv, dw_out = weight_grads(stage, normed_slice, grad_slice)
    return (grad_normed, dw_qkv, dw_out)


def solution(mesh):
    chips = Mesh(mesh.devices.reshape(4, 2, 4, 8), ("y", "core", "x", "z"))
    data = P(REC_AXES, None, FRAME_AXES)
    return jax.shard_map(
        body,
        mesh=chips,
        in_specs=(data, data, data, data, data, P(), P(), P(REC_AXES), P(REC_AXES)),
        out_specs=(data, P(FRAME_AXES, None), P(FRAME_AXES, None)),
        check_vma=False,
    )
```

```python
import math

import jax
import jax.numpy as jnp
from jax import lax
from jax.experimental import pallas as pl
from jax.experimental.pallas import tpu as pltpu
from jax.sharding import Mesh, PartitionSpec as P

HEAD_DIM = 32
HALF = 512
QT = 256
BLK = 128
GROUP = 4
UNROLL = 16
masked_score = -1e30
REC_AXES = ("y", "core")
FRAME_AXES = ("x", "z")
NT = (((1,), (1,)), ((), ()))


def attn_kernel(ids_ref, x_ref, out_ref, kv_t, k_p, v_p, acc):
    blocks = x_ref.shape[0]
    seq = blocks * BLK
    span = QT + 2 * HALF
    scale = 1.0 / math.sqrt(HEAD_DIM)
    live = ids_ref[0]
    f32, bf = jnp.float32, jnp.bfloat16

    zpad = jnp.zeros((HALF, BLK), bf)
    dead = jnp.where(lax.broadcasted_iota(jnp.int32, (HALF, BLK), 1) == HEAD_DIM, masked_score, 0.0).astype(bf)
    kv_t[0:HALF, :] = dead
    kv_t[HALF + seq :, :] = dead
    zl = jnp.zeros((HEAD_DIM, HALF), bf)
    for ref in (k_p, v_p):
        ref[:, 0:HALF] = zl
        ref[:, HALF + seq :] = zl
    acc[...] = jnp.zeros_like(acc)
    row_frame = lax.broadcasted_iota(jnp.int32, (HEAD_DIM, BLK), 1)
    row_id = lax.broadcasted_iota(jnp.int32, (HEAD_DIM, BLK), 0)

    def prep(b, _):
        start = pl.multiple_of(HALF + b * BLK, BLK)
        k_blk = x_ref[b, HEAD_DIM : 2 * HEAD_DIM, :]
        v_blk = x_ref[b, 2 * HEAD_DIM : 3 * HEAD_DIM, :]
        k_p[:, pl.ds(start, BLK)] = k_blk
        v_p[:, pl.ds(start, BLK)] = v_blk
        bias = jnp.where((row_id == 0) & (row_frame + b * BLK >= live), masked_score, 0.0)
        wide = jnp.concatenate(
            [k_blk.astype(f32), bias, v_blk.astype(f32), jnp.zeros((HEAD_DIM, BLK), f32)], axis=0
        )
        kv_t[pl.ds(start, BLK), :] = wide.T.astype(bf)
        return 0

    lax.fori_loop(0, blocks, prep, 0, unroll=UNROLL)

    b_id = lax.broadcasted_iota(jnp.int32, (QT, QT), 0)
    a_id = lax.broadcasted_iota(jnp.int32, (QT, QT), 1)
    ones_row = jnp.where(lax.broadcasted_iota(jnp.int32, (HEAD_DIM, QT), 0) == 0, 1.0, 0.0).astype(bf)
    z64 = jnp.zeros((2 * HEAD_DIM, QT), bf)
    z32 = jnp.zeros((HEAD_DIM, QT), bf)
    c = scale * math.log2(math.e)

    def dot(a, b):
        return jnp.dot(a, b, preferred_element_type=f32)

    below = b_id > a_id
    above = b_id < a_id

    def group(n, _):
        tiles = [n * GROUP + j for j in range(GROUP)]
        bases = [pl.multiple_of(i * QT, QT) for i in tiles]
        qs, gs = [], []
        for i in tiles:
            x0, x1 = x_ref[2 * i], x_ref[2 * i + 1]
            q = jnp.concatenate([x0[0:32], x1[0:32]], axis=1)
            g = jnp.concatenate([x0[96:128], x1[96:128]], axis=1)
            qs.append(jnp.concatenate([q, ones_row, z64], axis=0))
            gs.append(jnp.concatenate([z64, g, z32], axis=0))
        kvs = [kv_t[pl.ds(b, span), :] for b in bases]
        ss = [dot(kv, r) for kv, r in zip(kvs, qs)]
        pgs = [dot(kv, r) for kv, r in zip(kvs, gs)]
        mids, edges, ps, aos = [], [], [], []
        for j in range(GROUP):
            s = ss[j]
            edge = jnp.where(below, s[0:QT], jnp.where(above, s[span - QT :], masked_score))
            mid = s[QT : span - QT]
            m = jnp.maximum(jnp.max(mid, axis=0, keepdims=True), jnp.max(edge, axis=0, keepdims=True))
            mid = jnp.exp2((mid - m) * c)
            edge = jnp.exp2((edge - m) * c)
            total = jnp.sum(mid, axis=0, keepdims=True) + jnp.sum(edge, axis=0, keepdims=True)
            q_live = bases[j] + lax.broadcasted_iota(jnp.int32, (1, QT), 1) < live
            inv = jnp.where(q_live, 1.0 / total, 0.0)
            mid = mid * inv
            edge = edge * inv
            p = jnp.concatenate(
                [jnp.where(below, edge, 0.0).astype(bf), mid.astype(bf), jnp.where(above, edge, 0.0).astype(bf)],
                axis=0,
            )
            mids.append(mid)
            edges.append(edge)
            ps.append(p)
            aos.append(dot(v_p[:, pl.ds(bases[j], span)], p).astype(bf))
        dss, gqs = [], []
        for j in range(GROUP):
            pg = pgs[j]
            rd = jnp.sum(gs[j][64:96].astype(f32) * aos[j].astype(f32), axis=0, keepdims=True)
            d_mid = mids[j] * (pg[QT : span - QT] - rd)
            d_edge = edges[j] * (jnp.where(below, pg[0:QT], pg[span - QT :]) - rd)
            ds = jnp.concatenate(
                [jnp.where(below, d_edge, 0.0).astype(bf), d_mid.astype(bf), jnp.where(above, d_edge, 0.0).astype(bf)],
                axis=0,
            )
            dss.append(ds)
            gqs.append((dot(k_p[:, pl.ds(bases[j], span)], ds) * scale).astype(bf))
        for j in range(GROUP):
            acc[pl.ds(bases[j], span), :] += dot(dss[j], qs[j].T) + dot(ps[j], gs[j].T)
        for j in range(GROUP):
            for half in range(2):
                sl = slice(half * BLK, (half + 1) * BLK)
                out_ref[2 * tiles[j] + half, 0:32, :] = gqs[j][:, sl]
                out_ref[2 * tiles[j] + half, 96:128, :] = aos[j][:, sl]
        return 0

    lax.fori_loop(0, seq // QT // GROUP, group, 0)

    def flush(b, _):
        start = pl.multiple_of(HALF + b * BLK, BLK)
        t = acc[pl.ds(start, BLK), :].T
        out_ref[b, 32:64, :] = (t[0:32] * scale).astype(bf)
        out_ref[b, 64:96, :] = t[64:96].astype(bf)
        return 0

    lax.fori_loop(0, blocks, flush, 0, unroll=UNROLL)

def attention(x, ids):
    blocks = x.shape[0]
    seq = blocks * BLK
    padded = seq + 2 * HALF
    return pl.pallas_call(
        attn_kernel,
        out_shape=jax.ShapeDtypeStruct(x.shape, jnp.bfloat16),
        in_specs=[pl.BlockSpec(memory_space=pltpu.SMEM), pl.BlockSpec(memory_space=pltpu.VMEM)],
        out_specs=pl.BlockSpec(memory_space=pltpu.VMEM),
        scratch_shapes=[
            pltpu.VMEM((padded, BLK), jnp.bfloat16),
            pltpu.VMEM((HEAD_DIM, padded), jnp.bfloat16),
            pltpu.VMEM((HEAD_DIM, padded), jnp.bfloat16),
            pltpu.VMEM((padded, BLK), jnp.float32),
        ],
        compiler_params=pltpu.CompilerParams(vmem_limit_bytes=40 << 20),
        cost_estimate=pl.CostEstimate(
            flops=6 * 2 * seq * (QT + 2 * HALF) * HEAD_DIM, bytes_accessed=2 * x.size * 2, transcendentals=seq * 2 * HALF
        ),
        name="window_attention",
    )(ids, x)


def terms_kernel(ids_ref, stage_ref, gathered_ref, out_ref):
    own_x, own_core = ids_ref[1], ids_ref[2]
    nx, nz, rows, frames = stage_ref.shape
    width = gathered_ref.shape[1] // 2
    g_rows = 3 * HEAD_DIM
    f32, bf = jnp.float32, jnp.bfloat16

    def wide(ref_slice):
        return [
            jnp.concatenate([ref_slice(k), ref_slice(k + 1)], axis=1) for k in range(0, nz, 2)
        ]

    def product(lefts, rights):
        return sum(
            lax.dot_general(a, b, NT, preferred_element_type=f32) for a, b in zip(lefts, rights)
        )

    grads = wide(lambda k: stage_ref[:, k, :g_rows, :].reshape(nx * g_rows, frames))
    aos = wide(lambda k: stage_ref[:, k, g_rows:, :].reshape(nx * HEAD_DIM, frames))
    half = width // 2
    blocks = half // BLK
    for core in range(2):
        slot = lax.rem(core + own_core, 2)
        for pair in range(blocks // 2):
            start = core * half + pair * 2 * BLK
            total = product(grads, wide(lambda k: gathered_ref[k, start : start + 2 * BLK, :]))
            total = total.astype(bf).reshape(nx, g_rows, 2 * BLK)
            for x in range(nx):
                to = lax.rem(x - own_x + nx, nx)
                for j in range(2):
                    b = 2 * pair + j
                    out_ref[slot, to, b * g_rows : (b + 1) * g_rows, :] = total[
                        x, :, j * BLK : (j + 1) * BLK
                    ]
    per_x = width // nx
    sub = HEAD_DIM // 2
    for x in range(nx):
        to = lax.rem(x - own_x + nx, nx)
        start = width + x * per_x
        total = product(wide(lambda k: gathered_ref[k, start : start + per_x, :]), aos)
        total = total.astype(bf).reshape(nz, 2, sub, nx * HEAD_DIM)
        for core in range(2):
            out_ref[lax.rem(core + own_core, 2), to, blocks * g_rows :, :] = total[
                :, core
            ].reshape(nz * sub, nx * HEAD_DIM)


def input_grad_kernel(w_ref, back_ref, out_ref, buf):
    nz, nx = back_ref.shape[:2]
    width = w_ref.shape[0]
    for z in range(nz):
        for x in range(nx):
            start = (x * nz + z) * HEAD_DIM
            for i in range(3):
                buf[i, start : start + HEAD_DIM, :] = back_ref[
                    z, x, i * HEAD_DIM : (i + 1) * HEAD_DIM, :
                ]
    total = jnp.zeros((BLK, width), jnp.float32)
    for i in range(3):
        total += jnp.dot(
            buf[i].T, w_ref[:, i * width : (i + 1) * width], preferred_element_type=jnp.float32
        )
    out_ref[...] = total.T.astype(jnp.bfloat16)


def local_call(kernel, name, out_shape, flops, scratch, *args):
    size = sum(a.size * a.dtype.itemsize for a in args) + math.prod(out_shape) * 2
    spaces = [pltpu.SMEM if a.dtype == jnp.int32 else pltpu.VMEM for a in args]
    return pl.pallas_call(
        kernel,
        out_shape=jax.ShapeDtypeStruct(out_shape, jnp.bfloat16),
        in_specs=[pl.BlockSpec(memory_space=space) for space in spaces],
        out_specs=pl.BlockSpec(memory_space=pltpu.VMEM),
        scratch_shapes=scratch,
        compiler_params=pltpu.CompilerParams(vmem_limit_bytes=40 << 20),
        cost_estimate=pl.CostEstimate(flops=flops, bytes_accessed=size, transcendentals=0),
        name=name,
    )(*args)


def swap_cores(v):
    return lax.ppermute(v, "core", [(0, 1), (1, 0)])


def shift(v, axis, k):
    n = lax.axis_size(axis)
    return lax.ppermute(v, axis, [(i, (i + k) % n) for i in range(n)])


def add_up(*terms):
    terms = [t.astype(jnp.float32) for t in terms]
    while len(terms) > 1:
        terms = [a + b for a, b in zip(terms[::2], terms[1::2])]
    return terms[0].astype(jnp.bfloat16)


def weight_grads(terms, back, width):
    nz = lax.axis_size("z")
    core = lax.axis_index("core")
    mine = add_up(terms[0], swap_cores(terms[1]))
    mine = add_up(mine[0], shift(mine[2], "x", 2), shift(mine[1], "x", 1), shift(mine[3], "x", 3))
    mine = add_up(mine, shift(mine, "y", 2), shift(mine, "y", 1), shift(mine, "y", 3))
    g_rows = 3 * HEAD_DIM
    blocks = width // 2 // BLK
    sub = HEAD_DIM // 2

    def both(part):
        other = swap_cores(part)
        return jnp.where(core == 0, jnp.stack([part, other]), jnp.stack([other, part]))

    qkv = both(mine[: blocks * g_rows]).reshape(2, blocks, 3, HEAD_DIM, BLK)
    dw_qkv = qkv.transpose(3, 2, 0, 1, 4).reshape(HEAD_DIM, 3 * width).astype(jnp.float32)
    out = mine[blocks * g_rows :].reshape(nz, sub, BLK)
    out, back = lax.optimization_barrier((out, back))
    out = both(lax.all_to_all(out, "z", 0, 0, tiled=True))
    out = out.reshape(2, nz, sub, BLK // HEAD_DIM, HEAD_DIM)
    dw_out = out.transpose(0, 2, 3, 1, 4).reshape(2 * sub, width).astype(jnp.float32)
    return dw_qkv, dw_out, back


def body(normed, query_act, key_act, value_act, grad_out, w_qkv, w_out, lengths, offsets):
    f32, bf = jnp.float32, jnp.bfloat16
    nx, nz = lax.axis_size("x"), lax.axis_size("z")
    shards = nx * nz
    width = w_out.shape[0]
    frames = normed.shape[2]
    seq_len = frames * shards
    rows = 4 * HEAD_DIM
    live = jnp.clip(lengths[0] - offsets[0], 0, seq_len)
    ids = jnp.stack([live, lax.axis_index("x"), lax.axis_index("core")]).astype(jnp.int32)
    own_grad = grad_out[0]
    gathered = lax.all_gather(jnp.concatenate([normed[0], own_grad], axis=0), "z")
    head_grad = lax.dot_general(
        w_out, own_grad, (((0,), (0,)), ((), ())), preferred_element_type=f32
    ).astype(bf)
    sent = jnp.concatenate(
        [a.reshape(shards, HEAD_DIM, frames) for a in (query_act[0], key_act[0], value_act[0], head_grad)],
        axis=1,
    )
    heads = lax.all_to_all(sent, FRAME_AXES, 0, 0, tiled=True)
    grads = attention(heads, ids)

    stage = lax.all_to_all(grads.reshape(nx, nz, rows, frames), "x", 0, 0, tiled=True)
    back = lax.all_to_all(
        stage[:, :, : 3 * HEAD_DIM].transpose(1, 0, 2, 3), "z", 0, 0, tiled=True
    )
    terms = local_call(
        terms_kernel,
        "weight_grad_terms",
        (2, nx, width // 2 // BLK * 3 * HEAD_DIM + nz * HEAD_DIM // 2, BLK),
        2 * nx * rows * width * nz * frames,
        [],
        ids,
        stage,
        gathered,
    )
    dw_qkv, dw_out, back = weight_grads(terms, back, width)
    grad_normed = local_call(
        input_grad_kernel,
        "input_grad",
        (width, frames),
        6 * width * width * frames,
        [pltpu.VMEM((3, width, frames), bf)],
        w_qkv,
        back,
    )[None]
    return (grad_normed, dw_qkv, dw_out)


def solution(mesh):
    chips = Mesh(mesh.devices.reshape(4, 2, 4, 8), ("y", "core", "x", "z"))
    data = P(REC_AXES, None, FRAME_AXES)
    return jax.shard_map(
        body,
        mesh=chips,
        in_specs=(data, data, data, data, data, P(), P(), P(REC_AXES), P(REC_AXES)),
        out_specs=(data, P(FRAME_AXES, None), P(FRAME_AXES, None)),
        check_vma=False,
    )
```

```python
import math

import jax
import jax.numpy as jnp
from jax import lax
from jax.experimental import pallas as pl
from jax.experimental.pallas import tpu as pltpu
from jax.sharding import Mesh, PartitionSpec as P

HEAD_DIM = 32
HALF = 512
QT = 256
BLK = 128
GROUP = 4
UNROLL = 16
masked_score = -1e30
REC_AXES = ("y", "core")
FRAME_AXES = ("x", "z")
NT = (((1,), (1,)), ((), ()))


def attn_kernel(ids_ref, x_ref, *refs):
    parts, (gq_ref, ao_ref, kv_t, k_p, v_p, acc) = refs[:-6], refs[-6:]
    nx, nz = len(parts), parts[0].shape[0]
    own_x = ids_ref[1]
    blocks = x_ref.shape[0]
    seq = blocks * BLK
    span = QT + 2 * HALF
    scale = 1.0 / math.sqrt(HEAD_DIM)
    live = ids_ref[0]
    f32, bf = jnp.float32, jnp.bfloat16

    zpad = jnp.zeros((HALF, BLK), bf)
    dead = jnp.where(lax.broadcasted_iota(jnp.int32, (HALF, BLK), 1) == HEAD_DIM, masked_score, 0.0).astype(bf)
    kv_t[0:HALF, :] = dead
    kv_t[HALF + seq :, :] = dead
    zl = jnp.zeros((HEAD_DIM, HALF), bf)
    for ref in (k_p, v_p):
        ref[:, 0:HALF] = zl
        ref[:, HALF + seq :] = zl
    acc[...] = jnp.zeros_like(acc)
    row_frame = lax.broadcasted_iota(jnp.int32, (HEAD_DIM, BLK), 1)
    row_id = lax.broadcasted_iota(jnp.int32, (HEAD_DIM, BLK), 0)

    def prep(b, _):
        start = pl.multiple_of(HALF + b * BLK, BLK)
        k_blk = x_ref[b, HEAD_DIM : 2 * HEAD_DIM, :]
        v_blk = x_ref[b, 2 * HEAD_DIM : 3 * HEAD_DIM, :]
        k_p[:, pl.ds(start, BLK)] = k_blk
        v_p[:, pl.ds(start, BLK)] = v_blk
        bias = jnp.where((row_id == 0) & (row_frame + b * BLK >= live), masked_score, 0.0)
        wide = jnp.concatenate(
            [k_blk.astype(f32), bias, v_blk.astype(f32), jnp.zeros((HEAD_DIM, BLK), f32)], axis=0
        )
        kv_t[pl.ds(start, BLK), :] = wide.T.astype(bf)
        return 0

    lax.fori_loop(0, blocks, prep, 0, unroll=UNROLL)

    b_id = lax.broadcasted_iota(jnp.int32, (QT, QT), 0)
    a_id = lax.broadcasted_iota(jnp.int32, (QT, QT), 1)
    ones_row = jnp.where(lax.broadcasted_iota(jnp.int32, (HEAD_DIM, QT), 0) == 0, 1.0, 0.0).astype(bf)
    z64 = jnp.zeros((2 * HEAD_DIM, QT), bf)
    z32 = jnp.zeros((HEAD_DIM, QT), bf)
    c = scale * math.log2(math.e)

    def dot(a, b):
        return jnp.dot(a, b, preferred_element_type=f32)

    below = b_id > a_id
    above = b_id < a_id

    def group(n, _):
        tiles = [n * GROUP + j for j in range(GROUP)]
        bases = [pl.multiple_of(i * QT, QT) for i in tiles]
        qs, gs = [], []
        for i in tiles:
            x0, x1 = x_ref[2 * i], x_ref[2 * i + 1]
            q = jnp.concatenate([x0[0:32], x1[0:32]], axis=1)
            g = jnp.concatenate([x0[96:128], x1[96:128]], axis=1)
            qs.append(jnp.concatenate([q, ones_row, z64], axis=0))
            gs.append(jnp.concatenate([z64, g, z32], axis=0))
        kvs = [kv_t[pl.ds(b, span), :] for b in bases]
        ss = [dot(kv, r) for kv, r in zip(kvs, qs)]
        pgs = [dot(kv, r) for kv, r in zip(kvs, gs)]
        mids, edges, ps, aos = [], [], [], []
        for j in range(GROUP):
            s = ss[j]
            edge = jnp.where(below, s[0:QT], jnp.where(above, s[span - QT :], masked_score))
            mid = s[QT : span - QT]
            m = jnp.maximum(jnp.max(mid, axis=0, keepdims=True), jnp.max(edge, axis=0, keepdims=True))
            mid = jnp.exp2((mid - m) * c)
            edge = jnp.exp2((edge - m) * c)
            total = jnp.sum(mid, axis=0, keepdims=True) + jnp.sum(edge, axis=0, keepdims=True)
            q_live = bases[j] + lax.broadcasted_iota(jnp.int32, (1, QT), 1) < live
            inv = jnp.where(q_live, 1.0 / total, 0.0)
            mid = mid * inv
            edge = edge * inv
            p = jnp.concatenate(
                [jnp.where(below, edge, 0.0).astype(bf), mid.astype(bf), jnp.where(above, edge, 0.0).astype(bf)],
                axis=0,
            )
            mids.append(mid)
            edges.append(edge)
            ps.append(p)
            aos.append(dot(v_p[:, pl.ds(bases[j], span)], p).astype(bf))
        dss, gqs = [], []
        for j in range(GROUP):
            pg = pgs[j]
            rd = jnp.sum(gs[j][64:96].astype(f32) * aos[j].astype(f32), axis=0, keepdims=True)
            d_mid = mids[j] * (pg[QT : span - QT] - rd)
            d_edge = edges[j] * (jnp.where(below, pg[0:QT], pg[span - QT :]) - rd)
            ds = jnp.concatenate(
                [jnp.where(below, d_edge, 0.0).astype(bf), d_mid.astype(bf), jnp.where(above, d_edge, 0.0).astype(bf)],
                axis=0,
            )
            dss.append(ds)
            gqs.append((dot(k_p[:, pl.ds(bases[j], span)], ds) * scale).astype(bf))
        for j in range(GROUP):
            acc[pl.ds(bases[j], span), :] += dot(dss[j], qs[j].T) + dot(ps[j], gs[j].T)
        for j in range(GROUP):
            for half in range(2):
                sl = slice(half * BLK, (half + 1) * BLK)
                gq_ref[2 * tiles[j] + half] = gqs[j][:, sl]
                ao_ref[2 * tiles[j] + half] = aos[j][:, sl]
        return 0

    lax.fori_loop(0, seq // QT // GROUP, group, 0)

    for k in range(nx):
        for z in range(nz):
            b = lax.rem(own_x + k, nx) * nz + z
            start = pl.multiple_of(HALF + b * BLK, BLK)
            t = acc[pl.ds(start, BLK), :].T
            gk = (t[0:HEAD_DIM] * scale).astype(bf)
            gv = t[2 * HEAD_DIM : 3 * HEAD_DIM].astype(bf)
            parts[k][z] = jnp.concatenate([gq_ref[b], gk, gv, ao_ref[b]], axis=0)


def attention(x, ids, nx, nz):
    blocks = x.shape[0]
    seq = blocks * BLK
    padded = seq + 2 * HALF
    return kernel_call(
        attn_kernel,
        "window_attention",
        [pltpu.SMEM, pltpu.VMEM],
        [(nz, 4 * HEAD_DIM, BLK)] * nx,
        [
            pltpu.VMEM((blocks, HEAD_DIM, BLK), jnp.bfloat16),
            pltpu.VMEM((blocks, HEAD_DIM, BLK), jnp.bfloat16),
            pltpu.VMEM((padded, BLK), jnp.bfloat16),
            pltpu.VMEM((HEAD_DIM, padded), jnp.bfloat16),
            pltpu.VMEM((HEAD_DIM, padded), jnp.bfloat16),
            pltpu.VMEM((padded, BLK), jnp.float32),
        ],
        6 * 2 * seq * (QT + 2 * HALF) * HEAD_DIM,
        ids,
        x,
        exps=seq * 2 * HALF,
    )


def kernel_call(kernel, name, spaces, out_shapes, scratch, flops, *args, exps=0):
    outs = [jax.ShapeDtypeStruct(shape, jnp.bfloat16) for shape in out_shapes]
    return pl.pallas_call(
        kernel,
        out_shape=outs,
        in_specs=[pl.BlockSpec(memory_space=space) for space in spaces],
        out_specs=[pl.BlockSpec(memory_space=pltpu.VMEM)] * len(outs),
        scratch_shapes=scratch,
        compiler_params=pltpu.CompilerParams(vmem_limit_bytes=40 << 20),
        cost_estimate=pl.CostEstimate(
            flops=flops,
            bytes_accessed=sum(a.size * a.dtype.itemsize for a in args)
            + 2 * sum(math.prod(s) for s in out_shapes),
            transcendentals=exps,
        ),
        name=name,
    )(*args)


def terms_kernel(ids_ref, *refs):
    parts, (gathered_ref, mine_ref, other_ref, ao_ref) = refs[:-4], refs[-4:]
    own_x, own_core = ids_ref[1], ids_ref[2]
    nx = len(parts)
    nz, rows, frames = parts[0].shape
    width = gathered_ref.shape[1] // 2
    g_rows = 3 * HEAD_DIM
    f32, bf = jnp.float32, jnp.bfloat16
    chunk = 2 * BLK
    half = width // 2

    def wide(part):
        return [jnp.concatenate([part(k), part(k + 1)], axis=1) for k in range(0, nz, 2)]

    def gathered(start):
        return wide(lambda k: gathered_ref[k, pl.ds(start, chunk), :])

    def product(lefts, rights):
        return sum(
            lax.dot_general(a, b, NT, preferred_element_type=f32) for a, b in zip(lefts, rights)
        )

    for k in range(nx):
        ao_ref[lax.rem(own_x - k + nx, nx)] = parts[k][:, g_rows:, :]
    grads = wide(lambda z: jnp.concatenate([part[z, :g_rows, :] for part in parts], axis=0))
    aos = wide(lambda z: ao_ref[:, z].reshape(nx * HEAD_DIM, frames))
    chunks = half // chunk
    for slot, out_ref in ((1, other_ref), (0, mine_ref)):
        for n in range(chunks):
            start = pl.multiple_of(lax.rem(own_core + slot, 2) * half + n * chunk, chunk)
            total = product(grads, gathered(start)).astype(bf).reshape(nx, g_rows, chunk)
            for k in range(nx):
                for j in range(2):
                    b = n * 2 + j
                    out_ref[(nx - k) % nx, b * g_rows : (b + 1) * g_rows, :] = total[
                        k, :, j * BLK : (j + 1) * BLK
                    ]
    sub = HEAD_DIM // 2
    first = 2 * chunks * g_rows
    for x in range(nx):
        to = lax.rem(x - own_x + nx, nx)
        total = product(gathered(width + x * chunk), aos).reshape(nz, 2, sub, nx * HEAD_DIM)
        low, high = (total[:, core].reshape(nz * sub, nx * HEAD_DIM) for core in range(2))
        mine_ref[to, first:, :] = jnp.where(own_core == 0, low, high).astype(bf)
        other_ref[to, first:, :] = jnp.where(own_core == 0, high, low).astype(bf)


def weight_terms(ids, parts, gathered):
    nx = len(parts)
    nz, rows, frames = parts[0].shape
    width = gathered.shape[1] // 2
    out = (nx, width // 2 // BLK * 3 * HEAD_DIM + nz * HEAD_DIM // 2, BLK)
    return kernel_call(
        terms_kernel,
        "weight_grad_terms",
        [pltpu.SMEM] + [pltpu.VMEM] * (nx + 1),
        [out, out],
        [pltpu.VMEM((nx, nz, HEAD_DIM, frames), jnp.bfloat16)],
        2 * nx * rows * width * nz * frames,
        ids,
        *parts,
        gathered,
    )


def own_weights_kernel(ids_ref, w_ref, out_ref, buf, sems):
    own_x, own_z = ids_ref[1], ids_ref[3]
    nx, rows, cols = buf.shape
    width = out_ref.shape[0]
    nz = w_ref.shape[0] // rows // nx
    copies = []
    for k in range(nx):
        head = lax.rem(own_x - k + nx, nx) * nz + own_z
        start = pl.multiple_of(head * rows, rows)
        copies.append(
            pltpu.make_async_copy(w_ref.at[pl.ds(start, rows), :], buf.at[k], sems.at[k])
        )
    for copy in copies:
        copy.start()
    for copy in copies:
        copy.wait()
    own = jnp.concatenate(
        [buf[k, :, i * width : (i + 1) * width] for k in range(nx) for i in range(cols // width)],
        axis=0,
    )
    out_ref[...] = own.T


def own_weights(ids, w_qkv, nx):
    width, cols = w_qkv.shape
    return kernel_call(
        own_weights_kernel,
        "own_weights",
        [pltpu.SMEM, pl.ANY],
        [(width, nx * 3 * HEAD_DIM)],
        [pltpu.VMEM((nx, HEAD_DIM, cols), jnp.bfloat16), pltpu.SemaphoreType.DMA((nx,))],
        0,
        ids,
        w_qkv,
    )[0]


def input_terms_kernel(weights_ref, *refs):
    parts, out_ref = refs[:-1], refs[-1]
    g_rows = 3 * HEAD_DIM
    for z in range(0, out_ref.shape[0], 2):
        grads = jnp.concatenate(
            [
                jnp.concatenate([part[z + j, :g_rows, :] for part in parts], axis=0)
                for j in range(2)
            ],
            axis=1,
        )
        total = jnp.dot(weights_ref[...], grads, preferred_element_type=jnp.float32)
        total = total.astype(jnp.bfloat16)
        for j in range(2):
            out_ref[z + j] = total[:, j * BLK : (j + 1) * BLK]


def input_terms(weights, parts):
    width, rows = weights.shape
    nz = parts[0].shape[0]
    return kernel_call(
        input_terms_kernel,
        "input_terms",
        [pltpu.VMEM] * (1 + len(parts)),
        [(nz, width, BLK)],
        [],
        2 * width * rows * nz * BLK,
        weights,
        *parts,
    )[0]


def swap_cores(v):
    return lax.ppermute(v, "core", [(0, 1), (1, 0)])


def shift(v, axis, k):
    n = lax.axis_size(axis)
    return lax.ppermute(v, axis, [(i, (i + k) % n) for i in range(n)])


def add_up(*terms):
    terms = [t.astype(jnp.float32) for t in terms]
    while len(terms) > 1:
        terms = [a + b for a, b in zip(terms[::2], terms[1::2])]
    return terms[0].astype(jnp.bfloat16)


def sum_over_y(v):
    v = add_up(v, lax.ppermute(v, "y", [(0, 1), (1, 0), (2, 3), (3, 2)]))
    return add_up(v, lax.ppermute(v, "y", [(0, 3), (3, 0), (1, 2), (2, 1)]))


def weight_grads(mine, other, width):
    nz = lax.axis_size("z")
    core = lax.axis_index("core")
    mine = add_up(mine, swap_cores(other))
    mine = add_up(mine[0], shift(mine[2], "x", 2), shift(mine[1], "x", 1), shift(mine[3], "x", 3))
    rows = width // 2 // BLK * 3 * HEAD_DIM
    mine = sum_over_y(mine)

    def both(part):
        other = swap_cores(part)
        return jnp.where(core == 0, jnp.stack([part, other]), jnp.stack([other, part]))

    out = mine[rows:].reshape(nz, HEAD_DIM // 2, BLK)
    out = lax.all_to_all(out, "z", 0, 0, tiled=True)
    qkv = both(mine[:rows]).reshape(2, -1, 3, HEAD_DIM, BLK)
    dw_qkv = qkv.transpose(3, 2, 0, 1, 4).reshape(HEAD_DIM, 3 * width).astype(jnp.float32)
    out, dw_qkv = lax.optimization_barrier((out, dw_qkv))
    out = both(out).reshape(2, nz, HEAD_DIM // 2, BLK // HEAD_DIM, HEAD_DIM)
    dw_out = out.transpose(0, 2, 3, 1, 4).reshape(HEAD_DIM, width).astype(jnp.float32)
    return dw_qkv, dw_out


def body(normed, query_act, key_act, value_act, grad_out, w_qkv, w_out, lengths, offsets):
    f32, bf = jnp.float32, jnp.bfloat16
    nx, nz = lax.axis_size("x"), lax.axis_size("z")
    shards = nx * nz
    width = w_out.shape[0]
    frames = normed.shape[2]
    seq_len = frames * shards
    live = jnp.clip(lengths[0] - offsets[0], 0, seq_len)
    ids = jnp.stack([live] + [lax.axis_index(a) for a in ("x", "core", "z")]).astype(jnp.int32)
    own_grad = grad_out[0]
    head_grad = lax.dot_general(
        w_out, own_grad, (((0,), (0,)), ((), ())), preferred_element_type=f32
    ).astype(bf)
    sent = jnp.concatenate(
        [a.reshape(shards, HEAD_DIM, frames) for a in (query_act[0], key_act[0], value_act[0], head_grad)],
        axis=1,
    )
    heads = lax.all_to_all(sent, FRAME_AXES, 0, 0, tiled=True)
    own, _ = lax.optimization_barrier(((normed[0], own_grad), sent))
    gathered = lax.all_gather(jnp.concatenate(own, axis=0), "z")
    weights = own_weights(ids, w_qkv, nx)
    heads, weights = lax.optimization_barrier((heads, weights))
    parts = attention(heads, ids, nx, nz)
    parts = [parts[0]] + [shift(parts[k], "x", k) for k in range(1, nx)]
    terms = input_terms(weights, parts).reshape(nz * width, frames)
    grad_normed = lax.psum_scatter(terms, "z", scatter_dimension=0, tiled=True)
    mine, other = weight_terms(ids, parts, gathered)
    dw_qkv, dw_out = weight_grads(mine, other, width)
    return (grad_normed[None], dw_qkv, dw_out)


def solution(mesh):
    chips = Mesh(mesh.devices.reshape(4, 2, 4, 8), ("y", "core", "x", "z"))
    data = P(REC_AXES, None, FRAME_AXES)
    return jax.shard_map(
        body,
        mesh=chips,
        in_specs=(data, data, data, data, data, P(), P(), P(REC_AXES), P(REC_AXES)),
        out_specs=(data, P(FRAME_AXES, None), P(FRAME_AXES, None)),
        check_vma=False,
    )
```

```python
import math

import jax
import jax.numpy as jnp
from jax import lax
from jax.experimental import pallas as pl
from jax.experimental.pallas import tpu as pltpu
from jax.sharding import Mesh, PartitionSpec as P

HEAD_DIM = 32
HALF = 512
QT = 256
BLK = 128
GROUP = 4
UNROLL = 16
masked_score = -1e30
REC_AXES = ("y", "core")
FRAME_AXES = ("x", "z")
NT = (((1,), (1,)), ((), ()))


def attn_kernel(ids_ref, x_ref, *refs):
    parts, (gq_ref, ao_ref, kv_t, k_p, v_p, acc) = refs[:-6], refs[-6:]
    nx, nz = len(parts), parts[0].shape[0]
    own_x = ids_ref[1]

    def at(b):
        return lax.rem(b, nz) * nx + b // nz

    blocks = x_ref.shape[0]
    seq = blocks * BLK
    span = QT + 2 * HALF
    scale = 1.0 / math.sqrt(HEAD_DIM)
    live = ids_ref[0]
    f32, bf = jnp.float32, jnp.bfloat16

    zpad = jnp.zeros((HALF, BLK), bf)
    dead = jnp.where(lax.broadcasted_iota(jnp.int32, (HALF, BLK), 1) == HEAD_DIM, masked_score, 0.0).astype(bf)
    kv_t[0:HALF, :] = dead
    kv_t[HALF + seq :, :] = dead
    zl = jnp.zeros((HEAD_DIM, HALF), bf)
    for ref in (k_p, v_p):
        ref[:, 0:HALF] = zl
        ref[:, HALF + seq :] = zl
    acc[...] = jnp.zeros_like(acc)
    row_frame = lax.broadcasted_iota(jnp.int32, (HEAD_DIM, BLK), 1)
    row_id = lax.broadcasted_iota(jnp.int32, (HEAD_DIM, BLK), 0)

    def prep(b, _):
        start = pl.multiple_of(HALF + b * BLK, BLK)
        k_blk = x_ref[at(b), HEAD_DIM : 2 * HEAD_DIM, :]
        v_blk = x_ref[at(b), 2 * HEAD_DIM : 3 * HEAD_DIM, :]
        k_p[:, pl.ds(start, BLK)] = k_blk
        v_p[:, pl.ds(start, BLK)] = v_blk
        bias = jnp.where((row_id == 0) & (row_frame + b * BLK >= live), masked_score, 0.0)
        wide = jnp.concatenate(
            [k_blk.astype(f32), bias, v_blk.astype(f32), jnp.zeros((HEAD_DIM, BLK), f32)], axis=0
        )
        kv_t[pl.ds(start, BLK), :] = wide.T.astype(bf)
        return 0

    lax.fori_loop(0, blocks, prep, 0, unroll=UNROLL)

    b_id = lax.broadcasted_iota(jnp.int32, (QT, QT), 0)
    a_id = lax.broadcasted_iota(jnp.int32, (QT, QT), 1)
    ones_row = jnp.where(lax.broadcasted_iota(jnp.int32, (HEAD_DIM, QT), 0) == 0, 1.0, 0.0).astype(bf)
    z64 = jnp.zeros((2 * HEAD_DIM, QT), bf)
    z32 = jnp.zeros((HEAD_DIM, QT), bf)
    c = scale * math.log2(math.e)

    def dot(a, b):
        return jnp.dot(a, b, preferred_element_type=f32)

    below = b_id > a_id
    above = b_id < a_id

    def group(n, _):
        tiles = [n * GROUP + j for j in range(GROUP)]
        bases = [pl.multiple_of(i * QT, QT) for i in tiles]
        qs, gs = [], []
        for i in tiles:
            x0, x1 = x_ref[at(2 * i)], x_ref[at(2 * i + 1)]
            q = jnp.concatenate([x0[0:32], x1[0:32]], axis=1)
            g = jnp.concatenate([x0[96:128], x1[96:128]], axis=1)
            qs.append(jnp.concatenate([q, ones_row, z64], axis=0))
            gs.append(jnp.concatenate([z64, g, z32], axis=0))
        kvs = [kv_t[pl.ds(b, span), :] for b in bases]
        ss = [dot(kv, r) for kv, r in zip(kvs, qs)]
        pgs = [dot(kv, r) for kv, r in zip(kvs, gs)]
        mids, edges, ps, aos = [], [], [], []
        for j in range(GROUP):
            s = ss[j]
            edge = jnp.where(below, s[0:QT], jnp.where(above, s[span - QT :], masked_score))
            mid = s[QT : span - QT]
            m = jnp.maximum(jnp.max(mid, axis=0, keepdims=True), jnp.max(edge, axis=0, keepdims=True))
            mid = jnp.exp2((mid - m) * c)
            edge = jnp.exp2((edge - m) * c)
            total = jnp.sum(mid, axis=0, keepdims=True) + jnp.sum(edge, axis=0, keepdims=True)
            q_live = bases[j] + lax.broadcasted_iota(jnp.int32, (1, QT), 1) < live
            inv = jnp.where(q_live, 1.0 / total, 0.0)
            mid = mid * inv
            edge = edge * inv
            p = jnp.concatenate(
                [jnp.where(below, edge, 0.0).astype(bf), mid.astype(bf), jnp.where(above, edge, 0.0).astype(bf)],
                axis=0,
            )
            mids.append(mid)
            edges.append(edge)
            ps.append(p)
            aos.append(dot(v_p[:, pl.ds(bases[j], span)], p).astype(bf))
        dss, gqs = [], []
        for j in range(GROUP):
            pg = pgs[j]
            rd = jnp.sum(gs[j][64:96].astype(f32) * aos[j].astype(f32), axis=0, keepdims=True)
            d_mid = mids[j] * (pg[QT : span - QT] - rd)
            d_edge = edges[j] * (jnp.where(below, pg[0:QT], pg[span - QT :]) - rd)
            ds = jnp.concatenate(
                [jnp.where(below, d_edge, 0.0).astype(bf), d_mid.astype(bf), jnp.where(above, d_edge, 0.0).astype(bf)],
                axis=0,
            )
            dss.append(ds)
            gqs.append((dot(k_p[:, pl.ds(bases[j], span)], ds) * scale).astype(bf))
        for j in range(GROUP):
            acc[pl.ds(bases[j], span), :] += dot(dss[j], qs[j].T) + dot(ps[j], gs[j].T)
        for j in range(GROUP):
            for half in range(2):
                sl = slice(half * BLK, (half + 1) * BLK)
                gq_ref[2 * tiles[j] + half] = gqs[j][:, sl]
                ao_ref[2 * tiles[j] + half] = aos[j][:, sl]
        return 0

    lax.fori_loop(0, seq // QT // GROUP, group, 0)

    for k in range(nx):
        for z in range(nz):
            b = lax.rem(own_x + k, nx) * nz + z
            start = pl.multiple_of(HALF + b * BLK, BLK)
            t = acc[pl.ds(start, BLK), :].T
            gk = (t[0:HEAD_DIM] * scale).astype(bf)
            gv = t[2 * HEAD_DIM : 3 * HEAD_DIM].astype(bf)
            parts[k][z] = jnp.concatenate([gq_ref[b], gk, gv, ao_ref[b]], axis=0)


def attention(x, ids, nx, nz):
    blocks = x.shape[0]
    seq = blocks * BLK
    padded = seq + 2 * HALF
    return kernel_call(
        attn_kernel,
        "window_attention",
        [pltpu.SMEM, pltpu.VMEM],
        [(nz, 4 * HEAD_DIM, BLK)] * nx,
        [
            pltpu.VMEM((blocks, HEAD_DIM, BLK), jnp.bfloat16),
            pltpu.VMEM((blocks, HEAD_DIM, BLK), jnp.bfloat16),
            pltpu.VMEM((padded, BLK), jnp.bfloat16),
            pltpu.VMEM((HEAD_DIM, padded), jnp.bfloat16),
            pltpu.VMEM((HEAD_DIM, padded), jnp.bfloat16),
            pltpu.VMEM((padded, BLK), jnp.float32),
        ],
        6 * 2 * seq * (QT + 2 * HALF) * HEAD_DIM,
        ids,
        x,
        exps=seq * 2 * HALF,
    )


def kernel_call(kernel, name, spaces, out_shapes, scratch, flops, *args, exps=0):
    outs = [jax.ShapeDtypeStruct(shape, jnp.bfloat16) for shape in out_shapes]
    return pl.pallas_call(
        kernel,
        out_shape=outs,
        in_specs=[pl.BlockSpec(memory_space=space) for space in spaces],
        out_specs=[pl.BlockSpec(memory_space=pltpu.VMEM)] * len(outs),
        scratch_shapes=scratch,
        compiler_params=pltpu.CompilerParams(vmem_limit_bytes=40 << 20),
        cost_estimate=pl.CostEstimate(
            flops=flops,
            bytes_accessed=sum(a.size * a.dtype.itemsize for a in args)
            + 2 * sum(math.prod(s) for s in out_shapes),
            transcendentals=exps,
        ),
        name=name,
    )(*args)


def terms_kernel(ids_ref, *refs):
    parts, (gathered_ref, mine_ref, other_ref, ao_ref) = refs[:-4], refs[-4:]
    own_x, own_core = ids_ref[1], ids_ref[2]
    nx = len(parts)
    nz, rows, frames = parts[0].shape
    width = gathered_ref.shape[1] // 2
    g_rows = 3 * HEAD_DIM
    f32, bf = jnp.float32, jnp.bfloat16
    chunk = 2 * BLK
    half = width // 2

    def wide(part):
        return [jnp.concatenate([part(k), part(k + 1)], axis=1) for k in range(0, nz, 2)]

    def gathered(start):
        return wide(lambda k: gathered_ref[k, pl.ds(start, chunk), :])

    def product(lefts, rights):
        return sum(
            lax.dot_general(a, b, NT, preferred_element_type=f32) for a, b in zip(lefts, rights)
        )

    for k in range(nx):
        ao_ref[lax.rem(own_x - k + nx, nx)] = parts[k][:, g_rows:, :]
    grads = wide(lambda z: jnp.concatenate([part[z, :g_rows, :] for part in parts], axis=0))
    aos = wide(lambda z: ao_ref[:, z].reshape(nx * HEAD_DIM, frames))
    chunks = half // chunk
    for slot, out_ref in ((1, other_ref), (0, mine_ref)):
        for n in range(chunks):
            start = pl.multiple_of(lax.rem(own_core + slot, 2) * half + n * chunk, chunk)
            total = product(grads, gathered(start)).astype(bf).reshape(nx, g_rows, chunk)
            for k in range(nx):
                for j in range(2):
                    b = n * 2 + j
                    out_ref[(nx - k) % nx, b * g_rows : (b + 1) * g_rows, :] = total[
                        k, :, j * BLK : (j + 1) * BLK
                    ]
    sub = HEAD_DIM // 2
    first = 2 * chunks * g_rows
    for x in range(nx):
        to = lax.rem(x - own_x + nx, nx)
        total = product(gathered(width + x * chunk), aos).reshape(nz, 2, sub, nx * HEAD_DIM)
        low, high = (total[:, core].reshape(nz * sub, nx * HEAD_DIM) for core in range(2))
        mine_ref[to, first:, :] = jnp.where(own_core == 0, low, high).astype(bf)
        other_ref[to, first:, :] = jnp.where(own_core == 0, high, low).astype(bf)


def weight_terms(ids, parts, gathered):
    nx = len(parts)
    nz, rows, frames = parts[0].shape
    width = gathered.shape[1] // 2
    out = (nx, width // 2 // BLK * 3 * HEAD_DIM + nz * HEAD_DIM // 2, BLK)
    return kernel_call(
        terms_kernel,
        "weight_grad_terms",
        [pltpu.SMEM] + [pltpu.VMEM] * (nx + 1),
        [out, out],
        [pltpu.VMEM((nx, nz, HEAD_DIM, frames), jnp.bfloat16)],
        2 * nx * rows * width * nz * frames,
        ids,
        *parts,
        gathered,
    )


def own_weights_kernel(ids_ref, w_ref, out_ref, buf, sems):
    own_x, own_z = ids_ref[1], ids_ref[3]
    nx, rows, cols = buf.shape
    width = out_ref.shape[0]
    nz = w_ref.shape[0] // rows // nx
    copies = []
    for k in range(nx):
        head = lax.rem(own_x - k + nx, nx) * nz + own_z
        start = pl.multiple_of(head * rows, rows)
        copies.append(
            pltpu.make_async_copy(w_ref.at[pl.ds(start, rows), :], buf.at[k], sems.at[k])
        )
    for copy in copies:
        copy.start()
    for copy in copies:
        copy.wait()
    own = jnp.concatenate(
        [buf[k, :, i * width : (i + 1) * width] for k in range(nx) for i in range(cols // width)],
        axis=0,
    )
    out_ref[...] = own.T


def own_weights(ids, w_qkv, nx):
    width, cols = w_qkv.shape
    return kernel_call(
        own_weights_kernel,
        "own_weights",
        [pltpu.SMEM, pl.ANY],
        [(width, nx * 3 * HEAD_DIM)],
        [pltpu.VMEM((nx, HEAD_DIM, cols), jnp.bfloat16), pltpu.SemaphoreType.DMA((nx,))],
        0,
        ids,
        w_qkv,
    )[0]


def input_terms_kernel(weights_ref, *refs):
    parts, out_ref = refs[:-1], refs[-1]
    g_rows = 3 * HEAD_DIM
    for z in range(0, out_ref.shape[0], 2):
        grads = jnp.concatenate(
            [
                jnp.concatenate([part[z + j, :g_rows, :] for part in parts], axis=0)
                for j in range(2)
            ],
            axis=1,
        )
        total = jnp.dot(weights_ref[...], grads, preferred_element_type=jnp.float32)
        total = total.astype(jnp.bfloat16)
        for j in range(2):
            out_ref[z + j] = total[:, j * BLK : (j + 1) * BLK]


def input_terms(weights, parts):
    width, rows = weights.shape
    nz = parts[0].shape[0]
    return kernel_call(
        input_terms_kernel,
        "input_terms",
        [pltpu.VMEM] * (1 + len(parts)),
        [(nz, width, BLK)],
        [],
        2 * width * rows * nz * BLK,
        weights,
        *parts,
    )[0]


def swap_cores(v):
    return lax.ppermute(v, "core", [(0, 1), (1, 0)])


def shift(v, axis, k):
    n = lax.axis_size(axis)
    return lax.ppermute(v, axis, [(i, (i + k) % n) for i in range(n)])


def add_up(*terms):
    terms = [t.astype(jnp.float32) for t in terms]
    while len(terms) > 1:
        terms = [a + b for a, b in zip(terms[::2], terms[1::2])]
    return terms[0].astype(jnp.bfloat16)


def sum_over_y(v):
    v = add_up(v, lax.ppermute(v, "y", [(0, 1), (1, 0), (2, 3), (3, 2)]))
    return add_up(v, lax.ppermute(v, "y", [(0, 3), (3, 0), (1, 2), (2, 1)]))


def weight_grads(mine, other, width):
    nz = lax.axis_size("z")
    core = lax.axis_index("core")
    mine = add_up(mine, swap_cores(other))
    mine = add_up(mine[0], shift(mine[2], "x", 2), shift(mine[1], "x", 1), shift(mine[3], "x", 3))
    rows = width // 2 // BLK * 3 * HEAD_DIM
    mine = sum_over_y(mine)

    def both(part):
        other = swap_cores(part)
        return jnp.where(core == 0, jnp.stack([part, other]), jnp.stack([other, part]))

    out = mine[rows:].reshape(nz, HEAD_DIM // 2, BLK)
    out = lax.all_to_all(out, "z", 0, 0, tiled=True)
    qkv = both(mine[:rows]).reshape(2, -1, 3, HEAD_DIM, BLK)
    dw_qkv = qkv.transpose(3, 2, 0, 1, 4).reshape(HEAD_DIM, 3 * width).astype(jnp.float32)
    out, dw_qkv = lax.optimization_barrier((out, dw_qkv))
    out = both(out).reshape(2, nz, HEAD_DIM // 2, BLK // HEAD_DIM, HEAD_DIM)
    dw_out = out.transpose(0, 2, 3, 1, 4).reshape(HEAD_DIM, width).astype(jnp.float32)
    return dw_qkv, dw_out


def body(normed, query_act, key_act, value_act, grad_out, w_qkv, w_out, lengths, offsets):
    f32, bf = jnp.float32, jnp.bfloat16
    nx, nz = lax.axis_size("x"), lax.axis_size("z")
    shards = nx * nz
    width = w_out.shape[0]
    frames = normed.shape[2]
    seq_len = frames * shards
    live = jnp.clip(lengths[0] - offsets[0], 0, seq_len)
    ids = jnp.stack([live] + [lax.axis_index(a) for a in ("x", "core", "z")]).astype(jnp.int32)
    own_grad = grad_out[0]
    head_grad = lax.dot_general(
        w_out, own_grad, (((0,), (0,)), ((), ())), preferred_element_type=f32
    ).astype(bf)
    sent = jnp.concatenate(
        [a.reshape(nx, nz, HEAD_DIM, frames) for a in (query_act[0], key_act[0], value_act[0], head_grad)],
        axis=2,
    )
    sent = sent.transpose(1, 0, 2, 3).reshape(shards, 4 * HEAD_DIM, frames)
    heads = lax.all_to_all(sent, ("z", "x"), 0, 0, tiled=True)
    own, _ = lax.optimization_barrier(((normed[0], own_grad), sent))
    gathered = lax.all_gather(jnp.concatenate(own, axis=0), "z")
    weights = own_weights(ids, w_qkv, nx)
    heads, weights = lax.optimization_barrier((heads, weights))
    parts = attention(heads, ids, nx, nz)
    parts = [parts[0]] + [shift(parts[k], "x", k) for k in range(1, nx)]
    terms = input_terms(weights, parts).reshape(nz * width, frames)
    grad_normed = lax.psum_scatter(terms, "z", scatter_dimension=0, tiled=True)
    mine, other = weight_terms(ids, parts, gathered)
    dw_qkv, dw_out = weight_grads(mine, other, width)
    return (grad_normed[None], dw_qkv, dw_out)


def solution(mesh):
    chips = Mesh(mesh.devices.reshape(4, 2, 4, 8), ("y", "core", "x", "z"))
    data = P(REC_AXES, None, FRAME_AXES)
    return jax.shard_map(
        body,
        mesh=chips,
        in_specs=(data, data, data, data, data, P(), P(), P(REC_AXES), P(REC_AXES)),
        out_specs=(data, P(FRAME_AXES, None), P(FRAME_AXES, None)),
        check_vma=False,
    )
```

```python
import math

import jax
import jax.numpy as jnp
from jax import lax
from jax.experimental import pallas as pl
from jax.experimental.pallas import tpu as pltpu
from jax.sharding import Mesh, PartitionSpec as P

HEAD_DIM = 32
HALF = 512
QT = 256
BLK = 128
GROUP = 4
UNROLL = 16
masked_score = -1e30
REC_AXES = ("y", "core")
FRAME_AXES = ("x", "z")
NT = (((1,), (1,)), ((), ()))


def attn_kernel(ids_ref, x_ref, *refs):
    parts, (gq_ref, ao_ref, kv_t, k_p, v_p, acc) = refs[:-6], refs[-6:]
    nx, nz = len(parts), parts[0].shape[0]
    own_x = ids_ref[1]

    def at(b):
        return lax.rem(b, nz) * nx + b // nz

    blocks = x_ref.shape[0]
    seq = blocks * BLK
    span = QT + 2 * HALF
    scale = 1.0 / math.sqrt(HEAD_DIM)
    live = ids_ref[0]
    f32, bf = jnp.float32, jnp.bfloat16

    zpad = jnp.zeros((HALF, BLK), bf)
    dead = jnp.where(lax.broadcasted_iota(jnp.int32, (HALF, BLK), 1) == HEAD_DIM, masked_score, 0.0).astype(bf)
    kv_t[0:HALF, :] = dead
    kv_t[HALF + seq :, :] = dead
    zl = jnp.zeros((HEAD_DIM, HALF), bf)
    for ref in (k_p, v_p):
        ref[:, 0:HALF] = zl
        ref[:, HALF + seq :] = zl
    acc[...] = jnp.zeros_like(acc)
    row_frame = lax.broadcasted_iota(jnp.int32, (HEAD_DIM, BLK), 1)
    row_id = lax.broadcasted_iota(jnp.int32, (HEAD_DIM, BLK), 0)

    def prep(b, _):
        start = pl.multiple_of(HALF + b * BLK, BLK)
        k_blk = x_ref[at(b), HEAD_DIM : 2 * HEAD_DIM, :]
        v_blk = x_ref[at(b), 2 * HEAD_DIM : 3 * HEAD_DIM, :]
        k_p[:, pl.ds(start, BLK)] = k_blk
        v_p[:, pl.ds(start, BLK)] = v_blk
        bias = jnp.where((row_id == 0) & (row_frame + b * BLK >= live), masked_score, 0.0)
        wide = jnp.concatenate(
            [k_blk.astype(f32), bias, v_blk.astype(f32), jnp.zeros((HEAD_DIM, BLK), f32)], axis=0
        )
        kv_t[pl.ds(start, BLK), :] = wide.T.astype(bf)
        return 0

    lax.fori_loop(0, blocks, prep, 0, unroll=UNROLL)

    b_id = lax.broadcasted_iota(jnp.int32, (QT, QT), 0)
    a_id = lax.broadcasted_iota(jnp.int32, (QT, QT), 1)
    ones_row = jnp.where(lax.broadcasted_iota(jnp.int32, (HEAD_DIM, QT), 0) == 0, 1.0, 0.0).astype(bf)
    z64 = jnp.zeros((2 * HEAD_DIM, QT), bf)
    z32 = jnp.zeros((HEAD_DIM, QT), bf)
    c = scale * math.log2(math.e)

    def dot(a, b):
        return jnp.dot(a, b, preferred_element_type=f32)

    below = b_id > a_id
    above = b_id < a_id

    def group(n, _):
        tiles = [n * GROUP + j for j in range(GROUP)]
        bases = [pl.multiple_of(i * QT, QT) for i in tiles]
        qs, gs = [], []
        for i in tiles:
            x0, x1 = x_ref[at(2 * i)], x_ref[at(2 * i + 1)]
            q = jnp.concatenate([x0[0:32], x1[0:32]], axis=1)
            g = jnp.concatenate([x0[96:128], x1[96:128]], axis=1)
            qs.append(jnp.concatenate([q, ones_row, z64], axis=0))
            gs.append(jnp.concatenate([z64, g, z32], axis=0))
        kvs = [kv_t[pl.ds(b, span), :] for b in bases]
        ss = [dot(kv, r) for kv, r in zip(kvs, qs)]
        pgs = [dot(kv, r) for kv, r in zip(kvs, gs)]
        mids, edges, ps, aos = [], [], [], []
        for j in range(GROUP):
            s = ss[j]
            edge = jnp.where(below, s[0:QT], jnp.where(above, s[span - QT :], masked_score))
            mid = s[QT : span - QT]
            m = jnp.maximum(jnp.max(mid, axis=0, keepdims=True), jnp.max(edge, axis=0, keepdims=True))
            mid = jnp.exp2((mid - m) * c)
            edge = jnp.exp2((edge - m) * c)
            total = jnp.sum(mid, axis=0, keepdims=True) + jnp.sum(edge, axis=0, keepdims=True)
            q_live = bases[j] + lax.broadcasted_iota(jnp.int32, (1, QT), 1) < live
            inv = jnp.where(q_live, 1.0 / total, 0.0)
            mid = mid * inv
            edge = edge * inv
            p = jnp.concatenate(
                [jnp.where(below, edge, 0.0).astype(bf), mid.astype(bf), jnp.where(above, edge, 0.0).astype(bf)],
                axis=0,
            )
            mids.append(mid)
            edges.append(edge)
            ps.append(p)
            aos.append(dot(v_p[:, pl.ds(bases[j], span)], p).astype(bf))
        dss, gqs = [], []
        for j in range(GROUP):
            pg = pgs[j]
            rd = jnp.sum(gs[j][64:96].astype(f32) * aos[j].astype(f32), axis=0, keepdims=True)
            d_mid = mids[j] * (pg[QT : span - QT] - rd)
            d_edge = edges[j] * (jnp.where(below, pg[0:QT], pg[span - QT :]) - rd)
            ds = jnp.concatenate(
                [jnp.where(below, d_edge, 0.0).astype(bf), d_mid.astype(bf), jnp.where(above, d_edge, 0.0).astype(bf)],
                axis=0,
            )
            dss.append(ds)
            gqs.append((dot(k_p[:, pl.ds(bases[j], span)], ds) * scale).astype(bf))
        for j in range(GROUP):
            acc[pl.ds(bases[j], span), :] += dot(dss[j], qs[j].T) + dot(ps[j], gs[j].T)
        for j in range(GROUP):
            for half in range(2):
                sl = slice(half * BLK, (half + 1) * BLK)
                gq_ref[2 * tiles[j] + half] = gqs[j][:, sl]
                ao_ref[2 * tiles[j] + half] = aos[j][:, sl]
        return 0

    lax.fori_loop(0, seq // QT // GROUP, group, 0)

    for k in range(nx):
        for z in range(nz):
            b = lax.rem(own_x + k, nx) * nz + z
            start = pl.multiple_of(HALF + b * BLK, BLK)
            t = acc[pl.ds(start, BLK), :].T
            gk = (t[0:HEAD_DIM] * scale).astype(bf)
            gv = t[2 * HEAD_DIM : 3 * HEAD_DIM].astype(bf)
            parts[k][z] = jnp.concatenate([gq_ref[b], gk, gv, ao_ref[b]], axis=0)


def attention(x, ids, nx, nz):
    blocks = x.shape[0]
    seq = blocks * BLK
    padded = seq + 2 * HALF
    return kernel_call(
        attn_kernel,
        "window_attention",
        [pltpu.SMEM, pltpu.VMEM],
        [(nz, 4 * HEAD_DIM, BLK)] * nx,
        [
            pltpu.VMEM((blocks, HEAD_DIM, BLK), jnp.bfloat16),
            pltpu.VMEM((blocks, HEAD_DIM, BLK), jnp.bfloat16),
            pltpu.VMEM((padded, BLK), jnp.bfloat16),
            pltpu.VMEM((HEAD_DIM, padded), jnp.bfloat16),
            pltpu.VMEM((HEAD_DIM, padded), jnp.bfloat16),
            pltpu.VMEM((padded, BLK), jnp.float32),
        ],
        6 * 2 * seq * (QT + 2 * HALF) * HEAD_DIM,
        ids,
        x,
        exps=seq * 2 * HALF,
    )


def kernel_call(kernel, name, spaces, out_shapes, scratch, flops, *args, exps=0):
    outs = [jax.ShapeDtypeStruct(shape, jnp.bfloat16) for shape in out_shapes]
    return pl.pallas_call(
        kernel,
        out_shape=outs,
        in_specs=[pl.BlockSpec(memory_space=space) for space in spaces],
        out_specs=[pl.BlockSpec(memory_space=pltpu.VMEM)] * len(outs),
        scratch_shapes=scratch,
        compiler_params=pltpu.CompilerParams(vmem_limit_bytes=40 << 20),
        cost_estimate=pl.CostEstimate(
            flops=flops,
            bytes_accessed=sum(a.size * a.dtype.itemsize for a in args)
            + 2 * sum(math.prod(s) for s in out_shapes),
            transcendentals=exps,
        ),
        name=name,
    )(*args)


def terms_kernel(ids_ref, *refs):
    parts, (gathered_ref, mine_ref, other_ref, ao_ref) = refs[:-4], refs[-4:]
    own_x, own_core = ids_ref[1], ids_ref[2]
    nx = len(parts)
    nz, rows, frames = parts[0].shape
    width = gathered_ref.shape[1] // 2
    g_rows = 3 * HEAD_DIM
    f32, bf = jnp.float32, jnp.bfloat16
    chunk = 2 * BLK
    half = width // 2

    def wide(part):
        return [jnp.concatenate([part(k), part(k + 1)], axis=1) for k in range(0, nz, 2)]

    def gathered(start):
        return wide(lambda k: gathered_ref[k, pl.ds(start, chunk), :])

    def product(lefts, rights):
        return sum(
            lax.dot_general(a, b, NT, preferred_element_type=f32) for a, b in zip(lefts, rights)
        )

    for k in range(nx):
        ao_ref[lax.rem(own_x - k + nx, nx)] = parts[k][:, g_rows:, :]
    grads = wide(lambda z: jnp.concatenate([part[z, :g_rows, :] for part in parts], axis=0))
    aos = wide(lambda z: ao_ref[:, z].reshape(nx * HEAD_DIM, frames))
    chunks = half // chunk
    for slot, out_ref in ((1, other_ref), (0, mine_ref)):
        for n in range(chunks):
            start = pl.multiple_of(lax.rem(own_core + slot, 2) * half + n * chunk, chunk)
            total = product(grads, gathered(start)).astype(bf).reshape(nx, g_rows, chunk)
            for k in range(nx):
                for j in range(2):
                    b = n * 2 + j
                    out_ref[(nx - k) % nx, b * g_rows : (b + 1) * g_rows, :] = total[
                        k, :, j * BLK : (j + 1) * BLK
                    ]
    sub = HEAD_DIM // 2
    first = 2 * chunks * g_rows
    for x in range(nx):
        to = lax.rem(x - own_x + nx, nx)
        total = product(gathered(width + x * chunk), aos).reshape(nz, 2, sub, nx * HEAD_DIM)
        low, high = (total[:, core].reshape(nz * sub, nx * HEAD_DIM) for core in range(2))
        mine_ref[to, first:, :] = jnp.where(own_core == 0, low, high).astype(bf)
        other_ref[to, first:, :] = jnp.where(own_core == 0, high, low).astype(bf)


def weight_terms(ids, parts, gathered):
    nx = len(parts)
    nz, rows, frames = parts[0].shape
    width = gathered.shape[1] // 2
    out = (nx, width // 2 // BLK * 3 * HEAD_DIM + nz * HEAD_DIM // 2, BLK)
    return kernel_call(
        terms_kernel,
        "weight_grad_terms",
        [pltpu.SMEM] + [pltpu.VMEM] * (nx + 1),
        [out, out],
        [pltpu.VMEM((nx, nz, HEAD_DIM, frames), jnp.bfloat16)],
        2 * nx * rows * width * nz * frames,
        ids,
        *parts,
        gathered,
    )


def own_weights_kernel(ids_ref, w_ref, out_ref, buf, sems):
    own_x, own_z = ids_ref[1], ids_ref[3]
    nx, rows, cols = buf.shape
    width = out_ref.shape[0]
    nz = w_ref.shape[0] // rows // nx
    copies = []
    for k in range(nx):
        head = lax.rem(own_x - k + nx, nx) * nz + own_z
        start = pl.multiple_of(head * rows, rows)
        copies.append(
            pltpu.make_async_copy(w_ref.at[pl.ds(start, rows), :], buf.at[k], sems.at[k])
        )
    for copy in copies:
        copy.start()
    for copy in copies:
        copy.wait()
    own = jnp.concatenate(
        [buf[k, :, i * width : (i + 1) * width] for k in range(nx) for i in range(cols // width)],
        axis=0,
    )
    out_ref[...] = own.T


def own_weights(ids, w_qkv, nx):
    width, cols = w_qkv.shape
    return kernel_call(
        own_weights_kernel,
        "own_weights",
        [pltpu.SMEM, pl.ANY],
        [(width, nx * 3 * HEAD_DIM)],
        [pltpu.VMEM((nx, HEAD_DIM, cols), jnp.bfloat16), pltpu.SemaphoreType.DMA((nx,))],
        0,
        ids,
        w_qkv,
    )[0]


def input_terms_kernel(weights_ref, *refs):
    parts, out_ref = refs[:-1], refs[-1]
    g_rows = 3 * HEAD_DIM
    for z in range(0, out_ref.shape[0], 2):
        grads = jnp.concatenate(
            [
                jnp.concatenate([part[z + j, :g_rows, :] for part in parts], axis=0)
                for j in range(2)
            ],
            axis=1,
        )
        total = jnp.dot(weights_ref[...], grads, preferred_element_type=jnp.float32)
        total = total.astype(jnp.bfloat16)
        for j in range(2):
            out_ref[z + j] = total[:, j * BLK : (j + 1) * BLK]


def input_terms(weights, parts):
    width, rows = weights.shape
    nz = parts[0].shape[0]
    return kernel_call(
        input_terms_kernel,
        "input_terms",
        [pltpu.VMEM] * (1 + len(parts)),
        [(nz, width, BLK)],
        [],
        2 * width * rows * nz * BLK,
        weights,
        *parts,
    )[0]


def swap_cores(v):
    return lax.ppermute(v, "core", [(0, 1), (1, 0)])


def shift(v, axis, k):
    n = lax.axis_size(axis)
    return lax.ppermute(v, axis, [(i, (i + k) % n) for i in range(n)])


def add_up(*terms):
    terms = [t.astype(jnp.float32) for t in terms]
    while len(terms) > 1:
        terms = [a + b for a, b in zip(terms[::2], terms[1::2])]
    return terms[0].astype(jnp.bfloat16)


def sum_over_y(v):
    return add_up(v, shift(v, "y", 2), shift(v, "y", 1), shift(v, "y", 3))


def weight_grads(mine, other, width):
    nz = lax.axis_size("z")
    core = lax.axis_index("core")
    mine = add_up(mine, swap_cores(other))
    mine = add_up(mine[0], shift(mine[2], "x", 2), shift(mine[1], "x", 1), shift(mine[3], "x", 3))
    rows = width // 2 // BLK * 3 * HEAD_DIM
    mine = sum_over_y(mine)

    def both(part):
        other = swap_cores(part)
        return jnp.where(core == 0, jnp.stack([part, other]), jnp.stack([other, part]))

    out = mine[rows:].reshape(nz, HEAD_DIM // 2, BLK)
    out = lax.all_to_all(out, "z", 0, 0, tiled=True)
    qkv = both(mine[:rows]).reshape(2, -1, 3, HEAD_DIM, BLK)
    dw_qkv = qkv.transpose(3, 2, 0, 1, 4).reshape(HEAD_DIM, 3 * width).astype(jnp.float32)
    out, dw_qkv = lax.optimization_barrier((out, dw_qkv))
    out = both(out).reshape(2, nz, HEAD_DIM // 2, BLK // HEAD_DIM, HEAD_DIM)
    dw_out = out.transpose(0, 2, 3, 1, 4).reshape(HEAD_DIM, width).astype(jnp.float32)
    return dw_qkv, dw_out


def body(normed, query_act, key_act, value_act, grad_out, w_qkv, w_out, lengths, offsets):
    f32, bf = jnp.float32, jnp.bfloat16
    nx, nz = lax.axis_size("x"), lax.axis_size("z")
    shards = nx * nz
    width = w_out.shape[0]
    frames = normed.shape[2]
    seq_len = frames * shards
    live = jnp.clip(lengths[0] - offsets[0], 0, seq_len)
    ids = jnp.stack([live] + [lax.axis_index(a) for a in ("x", "core", "z")]).astype(jnp.int32)
    own_grad = grad_out[0]
    head_grad = lax.dot_general(
        w_out, own_grad, (((0,), (0,)), ((), ())), preferred_element_type=f32
    ).astype(bf)
    sent = jnp.concatenate(
        [a.reshape(nx, nz, HEAD_DIM, frames) for a in (query_act[0], key_act[0], value_act[0], head_grad)],
        axis=2,
    )
    sent = sent.transpose(1, 0, 2, 3).reshape(shards, 4 * HEAD_DIM, frames)
    heads = lax.all_to_all(sent, ("z", "x"), 0, 0, tiled=True)
    own, _ = lax.optimization_barrier(((normed[0], own_grad), sent))
    gathered = lax.all_gather(jnp.concatenate(own, axis=0), "z")
    weights = own_weights(ids, w_qkv, nx)
    heads, weights = lax.optimization_barrier((heads, weights))
    parts = attention(heads, ids, nx, nz)
    parts = [parts[0]] + [shift(parts[k], "x", k) for k in range(1, nx)]
    terms = input_terms(weights, parts).reshape(nz * width, frames)
    grad_normed = lax.psum_scatter(terms, "z", scatter_dimension=0, tiled=True)
    mine, other = weight_terms(ids, parts, gathered)
    dw_qkv, dw_out = weight_grads(mine, other, width)
    return (grad_normed[None], dw_qkv, dw_out)


def solution(mesh):
    chips = Mesh(mesh.devices.reshape(4, 2, 4, 8), ("y", "core", "x", "z"))
    data = P(REC_AXES, None, FRAME_AXES)
    return jax.shard_map(
        body,
        mesh=chips,
        in_specs=(data, data, data, data, data, P(), P(), P(REC_AXES), P(REC_AXES)),
        out_specs=(data, P(FRAME_AXES, None), P(FRAME_AXES, None)),
        check_vma=False,
    )
```
